32 devices in a mesh: rows: 16 (over z, y, x), cols: 2 (over core).
Axes of the slice: x: 2, y: 2, z: 4, core: 2. Of those that a mesh axis runs over, the one named last changes fastest.
Arguments:
- basis_t: bfloat16 [512, 65536], P('cols', 'rows'), may hold values from -0.75 to 0.75
- diag_tiles: bfloat16 [512, 128, 128], P('rows'), may hold values from -0.1875 to 0.1875
- off_tiles: bfloat16 [512, 8, 128, 128], P('rows'), may hold values from -0.1875 to 0.1875
- owners: int32 [512, 8], P('rows'), may hold values from 0 to 15, all different within a row; in each aligned block of 32 rows (0 to 31, 32 to 63, ...) at most 16 rows name the same one
- tile_block: int32 [512, 8], P('rows'), may hold values from 0 to 31
Outputs:
- reduced: float32 [512, 512], P('rows', 'cols')
The draws below stay inside these ranges and needn't reach their ends.
Inputs may be any that keep to these rules, and one draw needn't show every extreme that they name: Each block row names 8 different owners. Among the 32 block rows of one index of rows, no owner is named by more than 16 of them, a bound that some block reaches.
All inputs are finite; a program needn't handle non-finite values.
Results may differ from the reference program's by a relative error of at most 0.0029.
Values may be sent and summed in bfloat16 or wider, within the bound.
A program may use at most 128 MiB of HBM per device.

```python
import math
import jax
import jax.numpy as jnp
import numpy as np
from jax import lax

BS = 128
NV = 512
TPR = 8
BR_DEV = 32
CAP = 16
NB = 512
NODES = 65536
N_ROWS = 16


def with_ends(result, own_key, least, top_value):
    dims = result.shape
    place = [jax.random.randint(jax.random.fold_in(own_key, axis), (), 0, dims[axis]) for axis in range(len(dims))]
    result = result.at[tuple(place)].set(least)
    longest = dims.index(max(dims))
    place[longest] = (place[longest] + 1) % dims[longest]
    return result.at[tuple(place)].set(top_value)


def strengthened(values, stream_key, source, target, shards_of, factor):
    owner, partner = [(jnp.arange(values.shape[dim]) // (values.shape[dim] // shards_of)).reshape([-1 if axis == dim else 1 for axis in range(values.ndim)]) for dim in (source, target)]
    chosen = jax.random.permutation(stream_key, shards_of)[partner]
    strong = (owner == chosen) | (owner == (partner + shards_of // 2) % shards_of)
    return jnp.where(strong, factor * values, values)


def block_levels(stream_key, shape, shards, smallest, top_value):
    def one(position, blocks):
        heights = jax.random.uniform(jax.random.fold_in(jax.random.fold_in(stream_key, 6), position), (blocks,), jnp.float32, smallest / len(shards), top_value / len(shards))
        return jnp.repeat(jnp.exp(heights), shape[position] // blocks).reshape((-1,) + (1,) * (len(shape) - position - 1))

    gain = one(*shards[0])
    for cut in shards[1:]:
        gain = gain * one(*cut)
    return gain


def assign_block(rng, own, number, rows, number_of, top, reach, skew):
    sequence = jax.random.permutation(rng, number_of)
    packed, common = load_shares(number_of, rows * top, reach, skew, True), load_shares(number_of, rows * top, reach, skew, False)
    places = jnp.arange(number_of)

    def named(lengths, offset_by):
        used = int((lengths > 0).sum())
        fixed = max(1, used // 4)
        shifted = fixed + (places - fixed + offset_by * (used - fixed)) % max(1, number_of - fixed)
        return jnp.zeros((number_of,), jnp.int32).at[sequence[jnp.where(places < fixed, places, shifted)]].set(jnp.asarray(lengths, jnp.int32))

    lengths = jnp.where(number % 4 == 0, named(packed, number // 4), named(common, number - number // 4 - 1))
    mixed = jax.random.permutation(jax.random.fold_in(own, 3), number_of)
    giver, taker = mixed[0:number_of // 2 * 2:2], mixed[1:number_of // 2 * 2:2]
    slack = jnp.minimum(lengths[giver] - 1, reach - lengths[taker]) // 2
    slack = jnp.where((giver == sequence[0]) | (taker == sequence[0]) | (lengths[taker] == 0), 0, jnp.maximum(slack, 0))
    shifted = jax.random.randint(jax.random.fold_in(own, 4), (number_of // 2,), 0, 1 << 20) % (slack + 1)
    lengths = lengths.at[giver].add(-shifted).at[taker].add(shifted)
    members = jnp.searchsorted(jnp.cumsum(lengths), jnp.arange(rows * top), side="right").astype(jnp.int32)
    listing = members.reshape(top, rows).T
    listing = listing[jax.random.permutation(jax.random.fold_in(own, 1), rows)]
    offset_by = jax.random.randint(jax.random.fold_in(own, 2), (rows, 1), 0, top)
    return jnp.take_along_axis(listing, (jnp.arange(top)[None, :] + offset_by) % top, axis=1)


def load_shares(number_of, total, most, slope, full):
    loads = [(1 << 20) // math.isqrt(standing ** slope) + 1 for standing in range(1, number_of + 1)]
    largest = most if full else min(most, max(-(-total // number_of), total * loads[0] // sum(loads)))
    least = 1 if total - largest >= number_of - 1 else 0
    holding, spare = [largest] + [least] * (number_of - 1), total - largest - least * (number_of - 1)
    while spare > 0:
        candidates = [i for i in range(1, number_of) if holding[i] < largest] or [i for i in range(1, number_of) if holding[i] < most]
        whole, budget = sum([loads[i] for i in candidates]), spare
        for i in candidates:
            more = min(most - holding[i], max(1, budget * loads[i] // whole), spare)
            holding[i] = holding[i] + more
            spare = spare - more
    return np.array(holding)


def centred(key, shape, spread, most, pieces=(), held_as=jnp.bfloat16):
    result = spread * jax.random.normal(key, shape, jnp.float32)
    if pieces:
        result = result * block_levels(key, shape, pieces, -0.22, 0.18)
    return jnp.clip(result, -most, most).astype(held_as)


def gaussian_with(stream_key, shape, scale, bound, shards, heavy, held_as=jnp.bfloat16):
    result = scale * jax.random.normal(stream_key, shape, jnp.float32)
    if shards:
        result = result * block_levels(stream_key, shape, shards, -0.22, 0.18)
    return jnp.clip(strengthened(result, jax.random.fold_in(stream_key, 3), *heavy), -bound, bound).astype(held_as)


def setup_inputs(seed: int = 0) -> dict:
    key_of = jax.random.split(jax.random.key(seed), 6)
    basis_t = gaussian_with(key_of[0], (NV, NODES), BS ** -0.5, 0.75, ((0, 2), (1, 16)), (1, 0, 16, 2.0))
    diag_tiles = centred(key_of[1], (NB, BS, BS), (BS * (TPR + 1)) ** -0.5, 0.1875, ((0, 16),))
    off_tiles = centred(key_of[2], (NB, TPR, BS, BS), (BS * (TPR + 1)) ** -0.5, 0.1875, ((0, 16),))
    owners_keys = jax.random.split(jax.random.fold_in(key_of[3], 1), NB // BR_DEV)
    owners_turns = jax.random.permutation(jax.random.fold_in(key_of[3], 3), NB // BR_DEV)
    owners = jax.vmap(lambda own, number: assign_block(jax.random.fold_in(key_of[3], 2), own, number, BR_DEV, N_ROWS, TPR, CAP, 2))(owners_keys, owners_turns).reshape((NB, TPR))
    tile_block = with_ends(jax.random.randint(key_of[4], (NB, TPR), 0, BR_DEV), jax.random.fold_in(key_of[4], 1), 0, BR_DEV - 1).astype(jnp.int32)
    return dict(basis_t=basis_t, diag_tiles=diag_tiles, off_tiles=off_tiles, owners=owners, tile_block=tile_block)


def reference(basis_t, diag_tiles, off_tiles, owners, tile_block):
    blocks = basis_t.reshape(NV, NB, BS)
    block_col = (owners * BR_DEV + tile_block).astype(jnp.int32)

    def per_group(group_index):
        first = (group_index * BR_DEV).astype(jnp.int32)
        columns = lax.dynamic_slice_in_dim(block_col, first, BR_DEV, 0)
        panels = blocks[:, columns, :]
        couple = lax.dynamic_slice_in_dim(off_tiles, first, BR_DEV, 0)
        diagonal = lax.dynamic_slice_in_dim(diag_tiles, first, BR_DEV, 0)
        own_panels = lax.dynamic_slice_in_dim(blocks, first, BR_DEV, 1)
        image = jnp.einsum("cbkj,bkij->cbi", panels.astype(jnp.float32), couple.astype(jnp.float32))
        image = image + jnp.einsum("cbj,bij->cbi", own_panels.astype(jnp.float32), diagonal.astype(jnp.float32))
        image = image.astype(jnp.bfloat16).reshape(NV, BR_DEV * BS)
        return jnp.dot(own_panels.reshape(NV, BR_DEV * BS), image.T, preferred_element_type=jnp.float32)

    partial_sums = lax.map(per_group, jnp.arange(N_ROWS, dtype=jnp.int32))
    return jnp.sum(partial_sums, axis=0)
```

```python
import functools

import jax
import jax.numpy as jnp
from jax import lax
from jax.experimental import pallas as pl
from jax.experimental.pallas import tpu as pltpu
from jax.sharding import PartitionSpec as P

BS = 128
TPR = 8
PIECES = 4
MESH = pl.DeviceIdType.MESH
NT = (((1,), (1,)), ((), ()))
MIB = 1 << 20


def gather_kernel(
    n_rows, basis, off, diag, own, tile, vall, offp, diagp, ownp, tilep, pv, local_sem, send, recv, isend, irecv
):
    r, c = lax.axis_index("rows"), lax.axis_index("cols")
    x, y = r % 2, (r // 2) % 2
    width, nodes = basis.shape
    slab = width // 2
    rounds = 2 * PIECES
    piece = slab // PIECES
    rest = width // rounds
    half_rows = off.shape[0] // 2
    step_rows = half_rows // rounds
    lines = n_rows // 4
    side = r + 1 - 2 * x
    across = r + 2 - 4 * y
    twin = 1 - c
    z_kinds, y_kinds = lines - 1, lines
    Y0 = z_kinds
    XV = Y0 + y_kinds
    XA, XB, XD, CA, CB, CD, CO = range(XV + 1, XV + 8)

    barrier = pltpu.get_barrier_semaphore()
    friends = [(side, c), (across, c), (r, twin)] + [((r + 4 * d) % n_rows, c) for d in range(1, lines)]
    for friend in friends:
        pl.semaphore_signal(barrier, inc=1, device_id=friend, device_id_type=MESH)
    pl.semaphore_wait(barrier, len(friends))

    def copy(s, kind, src, dst, device):
        return pltpu.make_async_remote_copy(
            src_ref=src, dst_ref=dst, send_sem=send.at[s, kind], recv_sem=recv.at[s, kind],
            device_id=device, device_id_type=MESH,
        )

    def part(home, d, s):
        origin = (home - 4 * d + n_rows) % n_rows + (s // PIECES) * (1 - 2 * x)
        return vall.at[origin, pl.ds(pl.multiple_of((s % PIECES) * piece, piece), piece), :]

    def z_send(d, s):
        here = part(r, 0, s)
        return copy(s, d - 1, here, here, ((r + 4 * d) % n_rows, c))

    def z_recv(d, s):
        there = part(r, d, s)
        return copy(s, d - 1, there, there, (side, c))

    def y_send(d, s):
        here = part(r, d, s)
        return copy(s, Y0 + d, here, here, (across, c))

    def y_recv(d, s):
        there = part(across, d, s)
        return copy(s, Y0 + d, there, there, (across, c))

    def xv_send(s):
        rows = pl.multiple_of(s * piece, piece)
        src = basis.at[pl.ds(pl.multiple_of((1 - x) * slab + rows, piece), piece), :]
        return copy(s, XV, src, vall.at[r, pl.ds(rows, piece), :], (side, c))

    def xv_recv(s):
        dst = vall.at[side, pl.ds(pl.multiple_of(s * piece, piece), piece), :]
        return copy(s, XV, dst, dst, (side, c))

    def tiles(ref, core, s):
        return ref.at[pl.ds(core * half_rows + s * step_rows, step_rows)]

    def band(ref, s):
        return ref.at[pl.ds(pl.multiple_of(s * rest, rest), rest), :]

    def x_rest(s):
        return [
            copy(s, XA, tiles(off, c, s), tiles(offp, c, s), (side, c)),
            copy(s, XB, band(basis, s), band(pv.at[1], s), (side, c)),
            copy(s, XD, tiles(diag, c, s), tiles(diagp, c, s), (side, c)),
        ]

    def c_rest(s):
        return [
            copy(s, CA, tiles(offp, c, s), tiles(offp, c, s), (r, twin)),
            copy(s, CB, band(pv.at[1], s), band(pv.at[2], s), (r, twin)),
            copy(s, CD, tiles(diagp, c, s), tiles(diagp, c, s), (r, twin)),
        ]

    def c_recv(s):
        return [
            copy(s, CA, tiles(offp, twin, s), tiles(offp, twin, s), (r, twin)),
            copy(s, CB, band(pv.at[2], s), band(pv.at[2], s), (r, twin)),
            copy(s, CD, tiles(diagp, twin, s), tiles(diagp, twin, s), (r, twin)),
        ]

    def c_own(s):
        return copy(s, CO, band(basis, s), band(pv.at[0], s), (r, twin))

    keep = pltpu.make_async_copy(basis.at[pl.ds(pl.multiple_of(x * slab, slab), slab), :], vall.at[r], local_sem)
    keep.start()
    listed = [
        pltpu.make_async_remote_copy(
            src_ref=a, dst_ref=b, send_sem=isend.at[i], recv_sem=irecv.at[i], device_id=(side, c), device_id_type=MESH
        )
        for i, (a, b) in enumerate(((own, ownp), (tile, tilep)))
    ]
    for one in listed:
        one.start()
    keep.wait()

    def pass_on(s):
        for d in range(1, lines):
            z_recv(d, s).wait_recv()
            y_send(d, s).start()
        for came, go in zip(x_rest(s), c_rest(s)):
            came.wait_recv()
            go.start()

    @pl.loop(0, rounds)
    def _(s):
        @pl.when(s < PIECES)
        def _():
            xv_send(s).start()

        @pl.when(s >= PIECES)
        def _():
            xv_recv(s - PIECES).wait_recv()

        for d in range(1, lines):
            z_send(d, s).start()
        y_send(0, s).start()
        for one in x_rest(s):
            one.start()
        c_own(s).start()

        @pl.when(s >= 1)
        def _():
            pass_on(s - 1)

    pass_on(rounds - 1)

    @pl.loop(0, rounds)
    def _(s):
        for d in range(lines):
            y_recv(d, s).wait_recv()
            y_send(d, s).wait_send()
        for d in range(1, lines):
            z_send(d, s).wait_send()
        for one in c_recv(s):
            one.wait_recv()
        c_own(s).wait()
        for one in x_rest(s) + c_rest(s):
            one.wait_send()

        @pl.when(s < PIECES)
        def _():
            xv_send(s).wait_send()

    for one in listed:
        one.wait()


def gather(basis_t, diag, off, owners, tile_block):
    n_rows = lax.axis_size("rows")
    width, nodes = basis_t.shape
    rounds = 2 * PIECES
    kinds = (n_rows // 4 - 1) + n_rows // 4 + 8
    any_ = pl.BlockSpec(memory_space=pl.ANY)
    dma = pltpu.SemaphoreType.DMA
    return pl.pallas_call(
        functools.partial(gather_kernel, n_rows),
        out_shape=[
            jax.ShapeDtypeStruct((n_rows, width // 2, nodes), basis_t.dtype),
            jax.ShapeDtypeStruct(off.shape, off.dtype),
            jax.ShapeDtypeStruct(diag.shape, diag.dtype),
            jax.ShapeDtypeStruct(owners.shape, owners.dtype),
            jax.ShapeDtypeStruct(tile_block.shape, tile_block.dtype),
            jax.ShapeDtypeStruct((3, width, nodes), basis_t.dtype),
        ],
        in_specs=[any_] * 5,
        out_specs=[any_] * 6,
        scratch_shapes=[dma, dma((rounds, kinds)), dma((rounds, kinds)), dma((2,)), dma((2,))],
        compiler_params=pltpu.CompilerParams(collective_id=0, has_side_effects=True),
    )(basis_t, off, diag, owners, tile_block)


def project_kernel(groups, per_step, panel_counts, homes, *refs):
    n_panels = sum(panel_counts)
    lists = [refs[2 * g : 2 * g + 2] for g in range(groups)]
    vall = refs[2 * groups]
    blocks = [refs[2 * groups + 1 + 2 * g : 2 * groups + 3 + 2 * g] for g in range(groups)]
    start = 4 * groups + 1
    panels = refs[start : start + n_panels]
    out = refs[start + n_panels]
    step = pl.program_id(0)

    @pl.when(step == 0)
    def _():
        out[...] = jnp.zeros_like(out)

    done = 0
    for g in range(groups):
        (own, tile), (off, diag) = lists[g], blocks[g]
        images = []
        for i in range(per_step):
            b = step * per_step + i
            left = [
                vall[own[b, k], :, pl.ds(pl.multiple_of(tile[b, k] * BS, BS), BS)] for k in range(TPR)
            ] + [vall[homes[g], :, pl.ds(pl.multiple_of(b * BS, BS), BS)]]
            right = [off[i, k] for k in range(TPR)] + [diag[i]]
            images.append(
                lax.dot_general(
                    jnp.concatenate(left, axis=1),
                    jnp.concatenate(right, axis=1),
                    NT,
                    preferred_element_type=jnp.float32,
                ).astype(jnp.bfloat16)
            )
        image = jnp.concatenate(images, axis=1)
        row = 0
        for panel in panels[done : done + panel_counts[g]]:
            size = panel.shape[-2]
            values = panel[...].reshape(size, panel.shape[-1])
            out[pl.ds(row, size), :] += lax.dot_general(values, image, NT, preferred_element_type=jnp.float32)
            row += size
        done += panel_counts[g]


def project(homes, lists, vall, blocks, panels, per_step=4):
    groups = len(lists)
    local_rows = blocks[0][0].shape[0]
    total = sum(p.shape[-2] for p, _ in panels[0])
    smem = pl.BlockSpec(memory_space=pltpu.SMEM)
    span = per_step * BS
    args, specs = [homes], [smem]
    for pair in lists:
        args += pair
        specs += [smem, smem]
    args.append(vall)
    specs.append(pl.BlockSpec(vall.shape, lambda i: (0, 0, 0), pipeline_mode=pl.Buffered(1)))
    for off, diag in blocks:
        args += [off, diag]
        specs += [
            pl.BlockSpec((per_step, TPR, BS, BS), lambda i: (i, 0, 0, 0)),
            pl.BlockSpec((per_step, BS, BS), lambda i: (i, 0, 0)),
        ]
    for group in panels:
        for array, lead in group:
            args.append(array)
            if lead is None:
                specs.append(pl.BlockSpec((array.shape[0], span), lambda i: (0, i)))
            else:
                specs.append(pl.BlockSpec((1, array.shape[1], span), lambda i, lead=lead: (lead, 0, i)))
    width = vall.shape[1]
    return pl.pallas_call(
        functools.partial(project_kernel, groups, per_step, tuple(len(g) for g in panels)),
        out_shape=jax.ShapeDtypeStruct((total, width), jnp.float32),
        grid=(local_rows // per_step,),
        in_specs=specs,
        out_specs=pl.BlockSpec((total, width), lambda i: (0, 0)),
        compiler_params=pltpu.CompilerParams(vmem_limit_bytes=48 * MIB),
    )(*args)


def scatter_kernel(n_rows, partial, out, land, send, recv):
    r, c = lax.axis_index("rows"), lax.axis_index("cols")
    x = r % 2
    rows, width = out.shape[0], partial.shape[1]
    barrier = pltpu.get_barrier_semaphore()
    for d in range(1, n_rows):
        pl.semaphore_signal(barrier, inc=1, device_id=((r + d) % n_rows, c), device_id_type=MESH)
    pl.semaphore_wait(barrier, n_rows - 1)

    def share(target):
        per_half = n_rows // 2
        place = (target // per_half + c) % 2 * per_half + target % per_half
        return partial.at[pl.ds(pl.multiple_of(place * rows, rows), rows), :]

    def copy(d):
        target = (r + d) % n_rows
        return pltpu.make_async_remote_copy(
            src_ref=share(target), dst_ref=land.at[d], send_sem=send.at[d], recv_sem=recv.at[d],
            device_id=(target, c), device_id_type=MESH,
        )

    for d in range(1, n_rows):
        copy(d).start()
    mine = share(r)[...]
    other = jnp.zeros_like(mine)
    for d in range(1, n_rows):
        copy(d).wait_recv()
        if d % 2:
            other = other + land[d]
        else:
            mine = mine + land[d]
    first = x == 0
    out[:, pl.ds(0, width)] = jnp.where(first, mine, other)
    out[:, pl.ds(width, width)] = jnp.where(first, other, mine)
    for d in range(1, n_rows):
        copy(d).wait_send()


def scatter(partial):
    n_rows = lax.axis_size("rows")
    rows, width = partial.shape[0] // n_rows, partial.shape[1]
    dma = pltpu.SemaphoreType.DMA
    vmem = pl.BlockSpec(memory_space=pltpu.VMEM)
    return pl.pallas_call(
        functools.partial(scatter_kernel, n_rows),
        out_shape=jax.ShapeDtypeStruct((rows, 2 * width), jnp.float32),
        in_specs=[vmem],
        out_specs=vmem,
        scratch_shapes=[pltpu.VMEM((n_rows, rows, width), jnp.float32), dma((n_rows,)), dma((n_rows,))],
        compiler_params=pltpu.CompilerParams(collective_id=1, has_side_effects=True),
    )(partial)


def on_chip_pairs(basis_t, diag_tiles, off_tiles, owners, tile_block):
    vall, offp, diagp, ownp, tilep, pv = gather(basis_t, diag_tiles, off_tiles, owners, tile_block)
    r = lax.axis_index("rows")
    homes = jnp.stack([r, r + 1 - 2 * (r % 2)]).astype(jnp.int32)
    partial = project(
        homes,
        [(owners, tile_block), (ownp, tilep)],
        vall,
        [(off_tiles, diag_tiles), (offp, diagp)],
        [[(basis_t, None), (pv, 0)], [(pv, 1), (pv, 2)]],
    )
    return scatter(partial)


def general(basis_t, diag_tiles, off_tiles, owners, tile_block):
    vall = lax.all_gather(basis_t, "rows", axis=0, tiled=False)
    whole = lax.all_gather(basis_t, "cols", axis=0, tiled=True)
    homes = lax.axis_index("rows").astype(jnp.int32).reshape(1)
    partial = project(
        homes, [(owners, tile_block)], vall, [(off_tiles, diag_tiles)], [[(whole, None)]]
    )
    return lax.psum_scatter(partial, "rows", scatter_dimension=0, tiled=True)


def solution(mesh):
    in_specs = (
        P("cols", "rows"),
        P("rows", None, None),
        P("rows", None, None, None),
        P("rows", None),
        P("rows", None),
    )
    pairs = mesh.shape["cols"] == 2 and mesh.shape["rows"] % 4 == 0
    return jax.shard_map(
        on_chip_pairs if pairs else general,
        mesh=mesh, in_specs=in_specs, out_specs=P("rows", "cols"), check_vma=False,
    )
```

```python
import functools

import jax
import jax.numpy as jnp
from jax import lax
from jax.experimental import pallas as pl
from jax.experimental.pallas import tpu as pltpu
from jax.sharding import PartitionSpec as P

BS = 128
TPR = 8
LINE = 4
PIECES = 8
PIECE = 16
ROUNDS = 2 * PIECES
SWITCH = 13
KINDS = 16
FAMILY = 5
MESH = pl.DeviceIdType.MESH
NT = (((1,), (1,)), ((), ()))
MIB = 1 << 20


def START(copy):
    copy.start()


def WAIT_SEND(copy):
    copy.wait_send()


def gather_kernel(
    basis, off, diag, own, tile, vall, offp, diagp, ownp, tilep, pv0, pvx, pv2,
    local_sem, send, recv, bsend, brecv, isend, irecv,
):
    r, c = lax.axis_index("rows"), lax.axis_index("cols")
    x, y, z = r % 2, (r // 2) % 2, r // 4
    slab = basis.shape[0] // 2
    half_rows = off.shape[0] // 2
    side = r + 1 - 2 * x
    across = r + 2 - 4 * y
    twin = 1 - c
    FWD, Y0 = 4, 5
    XV, XA, XD, CA, CB, CD, CO = range(9, KINDS)

    barrier = pltpu.get_barrier_semaphore()
    friends = [(side, c), (across, c), (r, twin)] + [((r + 4 * d) % (4 * LINE), c) for d in range(1, LINE)]
    for friend in friends:
        pl.semaphore_signal(barrier, inc=1, device_id=friend, device_id_type=MESH)
    pl.semaphore_wait(barrier, len(friends))

    def remote(src, dst, ssem, rsem, device):
        return pltpu.make_async_remote_copy(
            src_ref=src, dst_ref=dst, send_sem=ssem, recv_sem=rsem, device_id=device, device_id_type=MESH
        )

    def copy(s, kind, src, dst, device):
        return remote(src, dst, send.at[s, kind], recv.at[s, kind], device)

    def band(ref, start):
        return ref.at[pl.ds(pl.multiple_of(start, PIECE), PIECE), :]

    def part(line, level, s):
        first = line * 4 + level * 2 + (x + s % 2) % 2
        return band(vall.at[first], (s // 2) * PIECE)

    def z_copy(family, s, target, origin, kind):
        here = part(origin, y if family == 0 else 1 - y, s)
        device = (target * 4 + r % 4, c)
        if family == 0:
            return copy_z(send.at[s, kind], recv.at[s, origin], here, device)
        return copy_z(bsend.at[s - SWITCH, kind], brecv.at[s - SWITCH, origin], here, device)

    def copy_z(ssem, rsem, here, device):
        return remote(here, here, ssem, rsem, device)

    def z_each(family, s, act):
        for t in range(LINE):
            near = (z != t) & (z - t <= 2) & (t - z <= 2)

            @pl.when(near)
            def _():
                act(z_copy(family, s, t, z, t))

    def z_forward(family, s, origin, act):
        if origin in (0, LINE - 1):
            @pl.when(z == (2 if origin == 0 else 1))
            def _():
                act(z_copy(family, s, LINE - 1 - origin, origin, FWD))

    def z_arrive(family, s, then):
        for o in range(LINE):
            @pl.when(z != o)
            def _():
                z_copy(family, s, (z + 1) % LINE, o, FWD).wait_recv()
                z_forward(family, s, o, START)
                then(o)

    def y_send(s, line):
        here = part(line, y, s)
        return copy(s, Y0 + line, here, here, (across, c))

    def y_recv(s, line):
        there = part(line, 1 - y, s)
        return copy(s, Y0 + line, there, there, (across, c))

    def xv_send(s):
        src = band(basis, (1 - x) * slab + s * PIECE)
        return copy(s, XV, src, band(vall.at[r], s * PIECE), (side, c))

    def xv_recv(s):
        dst = band(vall.at[side], s * PIECE)
        return copy(s, XV, dst, dst, (side, c))

    def xb(s):
        start = (s - PIECES) * PIECE
        return copy(s, XV, band(basis, x * slab + start), band(pvx, start), (side, c))

    def cb_vall(s):
        return copy(s, CB, band(vall.at[side], s * PIECE), band(pv2, x * slab + s * PIECE), (r, twin))

    def cb_rest(s):
        start = (s - PIECES) * PIECE
        return copy(s, CB, band(pvx, start), band(pv2, (1 - x) * slab + start), (r, twin))

    def x_tiles(s):
        at = c * half_rows + s
        return [
            copy(s, XA, off.at[at], offp.at[at], (side, c)),
            copy(s, XD, diag.at[at], diagp.at[at], (side, c)),
        ]

    def c_tiles(s, core):
        at = core * half_rows + s
        return [
            copy(s, CA, offp.at[at], offp.at[at], (r, twin)),
            copy(s, CD, diagp.at[at], diagp.at[at], (r, twin)),
        ]

    def c_own(s):
        return copy(s, CO, band(basis, s * PIECE), band(pv0, s * PIECE), (r, twin))

    keep = pltpu.make_async_copy(basis.at[pl.ds(pl.multiple_of(x * slab, slab), slab), :], vall.at[r], local_sem)
    keep.start()
    listed = [
        remote(a, b, isend.at[i], irecv.at[i], (side, c)) for i, (a, b) in enumerate(((own, ownp), (tile, tilep)))
    ]
    xv_send(0).start()
    for one in listed:
        one.start()
    keep.wait()

    def pass_on(s, late):
        def onward(o):
            if not late:
                y_send(s, o).start()

        z_arrive(0, s, onward)
        if late:
            z_arrive(1, s, lambda o: None)
        for came, go in zip(x_tiles(s), c_tiles(s, c)):
            came.wait_recv()
            go.start()

        @pl.when(s >= PIECES)
        def _():
            xb(s).wait_recv()
            cb_rest(s).start()

    def begin(s, late):
        @pl.when(s < PIECES - 1)
        def _():
            xv_send(s + 1).start()

        @pl.when((s >= 1) & (s <= PIECES))
        def _():
            xv_recv(s - 1).wait_recv()
            cb_vall(s - 1).start()

        if late:
            z_each(0, s, START)
            y_recv_late(s).wait_recv()
            z_each(1, s, START)
        else:
            z_each(0, s, START)
            y_send(s, z).start()

            @pl.when(s == PIECES + 1)
            def _():
                for later in range(SWITCH, ROUNDS):
                    y_send(later, z).start()
        for one in x_tiles(s):
            one.start()
        c_own(s).start()

        @pl.when(s >= PIECES)
        def _():
            xb(s).start()

    def y_recv_late(s):
        return y_recv(s, z)

    @pl.loop(0, SWITCH)
    def _(s):
        begin(s, False)

        @pl.when(s >= 1)
        def _():
            pass_on(s - 1, False)

    begin(SWITCH, True)
    pass_on(SWITCH - 1, False)

    @pl.loop(SWITCH + 1, ROUNDS)
    def _(s):
        begin(s, True)
        pass_on(s - 1, True)

    pass_on(ROUNDS - 1, True)

    @pl.loop(0, SWITCH)
    def _(s):
        for o in range(LINE):
            y_recv(s, o).wait_recv()
            y_send(s, o).wait_send()

    @pl.loop(SWITCH, ROUNDS)
    def _(s):
        y_send(s, z).wait_send()
        z_each(1, s, WAIT_SEND)
        for o in (0, LINE - 1):
            z_forward(1, s, o, WAIT_SEND)

    @pl.loop(0, ROUNDS)
    def _(s):
        z_each(0, s, WAIT_SEND)
        for o in (0, LINE - 1):
            z_forward(0, s, o, WAIT_SEND)
        for one in x_tiles(s) + c_tiles(s, c):
            one.wait_send()
        for one in c_tiles(s, twin):
            one.wait_recv()
        c_own(s).wait()

        @pl.when(s < PIECES)
        def _():
            xv_send(s).wait_send()
            cb_vall(s).wait()

        @pl.when(s >= PIECES)
        def _():
            xb(s).wait_send()
            cb_rest(s).wait()

    for one in listed:
        one.wait()


def gather(basis_t, diag, off, owners, tile_block):
    width, nodes = basis_t.shape
    any_ = pl.BlockSpec(memory_space=pl.ANY)
    dma = pltpu.SemaphoreType.DMA
    like = lambda a: jax.ShapeDtypeStruct(a.shape, a.dtype)
    return pl.pallas_call(
        gather_kernel,
        out_shape=[
            jax.ShapeDtypeStruct((4 * LINE, width // 2, nodes), basis_t.dtype),
            like(off), like(diag), like(owners), like(tile_block),
            like(basis_t),
            jax.ShapeDtypeStruct((width // 2, nodes), basis_t.dtype),
            like(basis_t),
        ],
        in_specs=[any_] * 5,
        out_specs=[any_] * 8,
        scratch_shapes=[
            dma, dma((ROUNDS, KINDS)), dma((ROUNDS, KINDS)),
            dma((ROUNDS - SWITCH, FAMILY)), dma((ROUNDS - SWITCH, FAMILY)), dma((2,)), dma((2,)),
        ],
        compiler_params=pltpu.CompilerParams(collective_id=0, has_side_effects=True),
    )(basis_t, off, diag, owners, tile_block)


def project_kernel(groups, per_step, panel_counts, homes, *refs):
    n_panels = sum(panel_counts)
    lists = [refs[2 * g : 2 * g + 2] for g in range(groups)]
    vall = refs[2 * groups]
    blocks = [refs[2 * groups + 1 + 2 * g : 2 * groups + 3 + 2 * g] for g in range(groups)]
    start = 4 * groups + 1
    panels = refs[start : start + n_panels]
    out = refs[start + n_panels]
    step = pl.program_id(0)

    @pl.when(step == 0)
    def _():
        out[...] = jnp.zeros_like(out)

    done = 0
    for g in range(groups):
        (own, tile), (off, diag) = lists[g], blocks[g]
        images = []
        for i in range(per_step):
            b = step * per_step + i
            left = [
                vall[own[b, k], :, pl.ds(pl.multiple_of(tile[b, k] * BS, BS), BS)] for k in range(TPR)
            ] + [vall[homes[g], :, pl.ds(pl.multiple_of(b * BS, BS), BS)]]
            right = [off[i, k] for k in range(TPR)] + [diag[i]]
            images.append(
                lax.dot_general(
                    jnp.concatenate(left, axis=1),
                    jnp.concatenate(right, axis=1),
                    NT,
                    preferred_element_type=jnp.float32,
                ).astype(jnp.bfloat16)
            )
        image = jnp.concatenate(images, axis=1)
        row = 0
        span = per_step * BS
        pieces = [p[...] for p in panels[done : done + panel_counts[g]]]
        starts = [None] * len(pieces)
        if g == 1:
            share = vall[homes[g], :, pl.ds(pl.multiple_of(step * span, span), span)]
            pieces = [share] + pieces
            size = share.shape[0]
            starts = [homes[2] * size, (1 - homes[2]) * size, 2 * size]
        for values, at in zip(pieces, starts):
            size = values.shape[0]
            place = pl.ds(row if at is None else pl.multiple_of(at, BS), size)
            out[place, :] += lax.dot_general(values, image, NT, preferred_element_type=jnp.float32)
            row += size
        done += panel_counts[g]


def project(homes, lists, vall, blocks, panels, per_step=4):
    groups = len(lists)
    local_rows = blocks[0][0].shape[0]
    total = sum(p.shape[0] for p in panels[0])
    smem = pl.BlockSpec(memory_space=pltpu.SMEM)
    span = per_step * BS
    args, specs = [homes], [smem]
    for pair in lists:
        args += pair
        specs += [smem, smem]
    args.append(vall)
    specs.append(pl.BlockSpec(vall.shape, lambda i: (0, 0, 0), pipeline_mode=pl.Buffered(1)))
    for off, diag in blocks:
        args += [off, diag]
        specs += [
            pl.BlockSpec((per_step, TPR, BS, BS), lambda i: (i, 0, 0, 0)),
            pl.BlockSpec((per_step, BS, BS), lambda i: (i, 0, 0)),
        ]
    for group in panels:
        for array in group:
            args.append(array)
            specs.append(pl.BlockSpec((array.shape[0], span), lambda i: (0, i)))
    width = vall.shape[1]
    return pl.pallas_call(
        functools.partial(project_kernel, groups, per_step, tuple(len(g) for g in panels)),
        out_shape=jax.ShapeDtypeStruct((total, width), jnp.float32),
        grid=(local_rows // per_step,),
        in_specs=specs,
        out_specs=pl.BlockSpec((total, width), lambda i: (0, 0)),
        compiler_params=pltpu.CompilerParams(vmem_limit_bytes=48 * MIB),
    )(*args)


def scatter_kernel(n_rows, partial, out, land, send, recv):
    r, c = lax.axis_index("rows"), lax.axis_index("cols")
    x = r % 2
    rows, width = out.shape[0], partial.shape[1]
    barrier = pltpu.get_barrier_semaphore()
    for d in range(1, n_rows):
        pl.semaphore_signal(barrier, inc=1, device_id=((r + d) % n_rows, c), device_id_type=MESH)
    pl.semaphore_wait(barrier, n_rows - 1)

    def share(target):
        per_half = n_rows // 2
        place = (target // per_half + c) % 2 * per_half + target % per_half
        return partial.at[pl.ds(pl.multiple_of(place * rows, rows), rows), :]

    def copy(d):
        target = (r + d) % n_rows
        return pltpu.make_async_remote_copy(
            src_ref=share(target), dst_ref=land.at[d], send_sem=send.at[d], recv_sem=recv.at[d],
            device_id=(target, c), device_id_type=MESH,
        )

    for d in range(1, n_rows):
        copy(d).start()
    mine = share(r)[...]
    other = jnp.zeros_like(mine)
    for d in range(1, n_rows):
        copy(d).wait_recv()
        if d % 2:
            other = other + land[d]
        else:
            mine = mine + land[d]
    first = x == 0
    out[:, pl.ds(0, width)] = jnp.where(first, mine, other)
    out[:, pl.ds(width, width)] = jnp.where(first, other, mine)
    for d in range(1, n_rows):
        copy(d).wait_send()


def scatter(partial):
    n_rows = lax.axis_size("rows")
    rows, width = partial.shape[0] // n_rows, partial.shape[1]
    dma = pltpu.SemaphoreType.DMA
    vmem = pl.BlockSpec(memory_space=pltpu.VMEM)
    return pl.pallas_call(
        functools.partial(scatter_kernel, n_rows),
        out_shape=jax.ShapeDtypeStruct((rows, 2 * width), jnp.float32),
        in_specs=[vmem],
        out_specs=vmem,
        scratch_shapes=[pltpu.VMEM((n_rows, rows, width), jnp.float32), dma((n_rows,)), dma((n_rows,))],
        compiler_params=pltpu.CompilerParams(collective_id=1, has_side_effects=True),
    )(partial)


def on_chip_pairs(basis_t, diag_tiles, off_tiles, owners, tile_block):
    vall, offp, diagp, ownp, tilep, pv0, pvx, pv2 = gather(basis_t, diag_tiles, off_tiles, owners, tile_block)
    r = lax.axis_index("rows")
    x = r % 2
    side = r + 1 - 2 * x
    homes = jnp.stack([r, side, x]).astype(jnp.int32)
    partial = project(
        homes,
        [(owners, tile_block), (ownp, tilep)],
        vall,
        [(off_tiles, diag_tiles), (offp, diagp)],
        [[basis_t, pv0], [pvx, pv2]],
    )
    return scatter(partial)


def general(basis_t, diag_tiles, off_tiles, owners, tile_block):
    vall = lax.all_gather(basis_t, "rows", axis=0, tiled=False)
    whole = lax.all_gather(basis_t, "cols", axis=0, tiled=True)
    homes = lax.axis_index("rows").astype(jnp.int32).reshape(1)
    partial = project(
        homes, [(owners, tile_block)], vall, [(off_tiles, diag_tiles)], [[whole]]
    )
    return lax.psum_scatter(partial, "rows", scatter_dimension=0, tiled=True)


def solution(mesh):
    in_specs = (
        P("cols", "rows"),
        P("rows", None, None),
        P("rows", None, None, None),
        P("rows", None),
        P("rows", None),
    )
    pairs = mesh.shape["cols"] == 2 and mesh.shape["rows"] == 4 * LINE
    return jax.shard_map(
        on_chip_pairs if pairs else general,
        mesh=mesh, in_specs=in_specs, out_specs=P("rows", "cols"), check_vma=False,
    )
```

```python
import functools

import jax
import jax.numpy as jnp
from jax import lax
from jax.experimental import pallas as pl
from jax.experimental.pallas import tpu as pltpu
from jax.sharding import PartitionSpec as P

BS = 128
TPR = 8
LINE = 4
PIECES = 8
PIECE = 16
ROUNDS = 2 * PIECES
SWITCH = 13
LAG = 2
KINDS = 16
FAMILY = 5
PER_STEP = 8
MESH = pl.DeviceIdType.MESH
NT = (((1,), (1,)), ((), ()))
MIB = 1 << 20


def START(copy):
    copy.start()


def WAIT_SEND(copy):
    copy.wait_send()


def gather_kernel(
    basis, off, diag, own, tile, vall, offp, diagp, ownp, tilep, pv0, pvx, pv2,
    stage, local_sem, send, recv, bsend, brecv, isend, irecv,
):
    r, c = lax.axis_index("rows"), lax.axis_index("cols")
    x, y, z = r % 2, (r // 2) % 2, r // 4
    slab = basis.shape[0] // 2
    half_rows = off.shape[0] // 2
    side = r + 1 - 2 * x
    across = r + 2 - 4 * y
    twin = 1 - c
    FWD, Y0 = 4, 5
    XV, XA, XD, CA, CB, CD, CO = range(9, KINDS)

    load = pltpu.make_async_copy(basis.at[pl.ds(pl.multiple_of(x * slab, slab), slab), :], stage, local_sem.at[0])
    keep = pltpu.make_async_copy(stage, vall.at[r], local_sem.at[1])
    load.start()

    barrier = pltpu.get_barrier_semaphore()
    friends = [(side, c), (across, c), (r, twin)] + [((r + 4 * d) % (4 * LINE), c) for d in range(1, LINE)]
    for friend in friends:
        pl.semaphore_signal(barrier, inc=1, device_id=friend, device_id_type=MESH)
    pl.semaphore_wait(barrier, len(friends))

    def remote(src, dst, ssem, rsem, device):
        return pltpu.make_async_remote_copy(
            src_ref=src, dst_ref=dst, send_sem=ssem, recv_sem=rsem, device_id=device, device_id_type=MESH
        )

    def copy(s, kind, src, dst, device):
        return remote(src, dst, send.at[s, kind], recv.at[s, kind], device)

    def band(ref, start):
        return ref.at[pl.ds(pl.multiple_of(start, PIECE), PIECE), :]

    def part(line, level, s):
        first = line * 4 + level * 2 + (x + s % 2) % 2
        return band(vall.at[first], (s // 2) * PIECE)

    def z_copy(family, s, target, origin, kind):
        here = part(origin, y if family == 0 else 1 - y, s)
        device = (target * 4 + r % 4, c)
        if family == 0:
            return copy_z(send.at[s, kind], recv.at[s, origin], here, device)
        return copy_z(bsend.at[s - SWITCH, kind], brecv.at[s - SWITCH, origin], here, device)

    def copy_z(ssem, rsem, here, device):
        return remote(here, here, ssem, rsem, device)

    def z_each(family, s, act):
        for t in range(LINE):
            near = (z != t) & (z - t <= 2) & (t - z <= 2)

            @pl.when(near)
            def _():
                act(z_copy(family, s, t, z, t))

    def z_forward(family, s, origin, act):
        if origin in (0, LINE - 1):
            @pl.when(z == (2 if origin == 0 else 1))
            def _():
                act(z_copy(family, s, LINE - 1 - origin, origin, FWD))

    def z_arrive(family, s, then):
        for o in range(LINE):
            @pl.when(z != o)
            def _():
                z_copy(family, s, (z + 1) % LINE, o, FWD).wait_recv()
                z_forward(family, s, o, START)
                then(o)

    def y_send(s, line):
        here = part(line, y, s)
        return copy(s, Y0 + line, here, here, (across, c))

    def y_recv(s, line):
        there = part(line, 1 - y, s)
        return copy(s, Y0 + line, there, there, (across, c))

    def xv_send(s):
        src = band(basis, (1 - x) * slab + s * PIECE)
        return copy(s, XV, src, band(vall.at[r], s * PIECE), (side, c))

    def xv_recv(s):
        dst = band(vall.at[side], s * PIECE)
        return copy(s, XV, dst, dst, (side, c))

    def xb(s):
        start = (s - PIECES) * PIECE
        return copy(s, XV, band(basis, x * slab + start), band(pvx, start), (side, c))

    def cb_vall(s):
        return copy(s, CB, band(vall.at[side], s * PIECE), band(pv2, x * slab + s * PIECE), (r, twin))

    def cb_rest(s):
        start = (s - PIECES) * PIECE
        return copy(s, CB, band(pvx, start), band(pv2, (1 - x) * slab + start), (r, twin))

    def x_tiles(s):
        at = c * half_rows + s
        return [
            copy(s, XA, off.at[at], offp.at[at], (side, c)),
            copy(s, XD, diag.at[at], diagp.at[at], (side, c)),
        ]

    def c_tiles(s, core):
        at = core * half_rows + s
        return [
            copy(s, CA, offp.at[at], offp.at[at], (r, twin)),
            copy(s, CD, diagp.at[at], diagp.at[at], (r, twin)),
        ]

    def c_own(s):
        return copy(s, CO, band(basis, s * PIECE), band(pv0, s * PIECE), (r, twin))

    listed = [
        remote(a, b, isend.at[i], irecv.at[i], (side, c)) for i, (a, b) in enumerate(((own, ownp), (tile, tilep)))
    ]
    xv_send(0).start()
    for one in listed:
        one.start()
    load.wait()
    keep.start()
    keep.wait()

    def pass_on(s, late):
        def onward(o):
            if not late:
                y_send(s, o).start()

        z_arrive(0, s, onward)
        if late:
            z_arrive(1, s, lambda o: None)
        for came, go in zip(x_tiles(s), c_tiles(s, c)):
            came.wait_recv()
            go.start()

        @pl.when(s >= PIECES)
        def _():
            xb(s).wait_recv()
            cb_rest(s).start()

    def begin(s, late):
        @pl.when(s < PIECES - 1)
        def _():
            xv_send(s + 1).start()

        @pl.when((s >= 1) & (s <= PIECES))
        def _():
            xv_recv(s - 1).wait_recv()
            cb_vall(s - 1).start()

        if late:
            z_each(0, s, START)
            y_recv_late(s).wait_recv()
            z_each(1, s, START)
        else:
            z_each(0, s, START)
            y_send(s, z).start()

            @pl.when(s == PIECES + 1)
            def _():
                for later in range(SWITCH, ROUNDS):
                    y_send(later, z).start()
        for one in x_tiles(s):
            one.start()
        c_own(s).start()

        @pl.when(s >= PIECES)
        def _():
            xb(s).start()

    def y_recv_late(s):
        return y_recv(s, z)

    @pl.loop(0, SWITCH)
    def _(s):
        begin(s, False)

        @pl.when(s >= LAG)
        def _():
            pass_on(s - LAG, False)

    for s in range(SWITCH, ROUNDS + LAG):
        if s < ROUNDS:
            begin(s, True)
        pass_on(s - LAG, s - LAG >= SWITCH)

    @pl.loop(0, SWITCH)
    def _(s):
        for o in range(LINE):
            y_recv(s, o).wait_recv()
            y_send(s, o).wait_send()

    @pl.loop(SWITCH, ROUNDS)
    def _(s):
        y_send(s, z).wait_send()
        z_each(1, s, WAIT_SEND)
        for o in (0, LINE - 1):
            z_forward(1, s, o, WAIT_SEND)

    @pl.loop(0, ROUNDS)
    def _(s):
        z_each(0, s, WAIT_SEND)
        for o in (0, LINE - 1):
            z_forward(0, s, o, WAIT_SEND)
        for one in x_tiles(s) + c_tiles(s, c):
            one.wait_send()
        for one in c_tiles(s, twin):
            one.wait_recv()
        c_own(s).wait()

        @pl.when(s < PIECES)
        def _():
            xv_send(s).wait_send()
            cb_vall(s).wait()

        @pl.when(s >= PIECES)
        def _():
            xb(s).wait_send()
            cb_rest(s).wait()

    for one in listed:
        one.wait()


def gather(basis_t, diag, off, owners, tile_block):
    width, nodes = basis_t.shape
    any_ = pl.BlockSpec(memory_space=pl.ANY)
    dma = pltpu.SemaphoreType.DMA
    like = lambda a: jax.ShapeDtypeStruct(a.shape, a.dtype)
    return pl.pallas_call(
        gather_kernel,
        out_shape=[
            jax.ShapeDtypeStruct((4 * LINE, width // 2, nodes), basis_t.dtype),
            like(off), like(diag), like(owners), like(tile_block),
            like(basis_t),
            jax.ShapeDtypeStruct((width // 2, nodes), basis_t.dtype),
            like(basis_t),
        ],
        in_specs=[any_] * 5,
        out_specs=[any_] * 8,
        scratch_shapes=[
            pltpu.VMEM((width // 2, nodes), basis_t.dtype), dma((2,)), dma((ROUNDS, KINDS)), dma((ROUNDS, KINDS)),
            dma((ROUNDS - SWITCH, FAMILY)), dma((ROUNDS - SWITCH, FAMILY)), dma((2,)), dma((2,)),
        ],
        compiler_params=pltpu.CompilerParams(collective_id=0, has_side_effects=True),
    )(basis_t, off, diag, owners, tile_block)


def project_kernel(groups, per_step, panel_counts, homes, *refs):
    n_panels = sum(panel_counts)
    lists = [refs[2 * g : 2 * g + 2] for g in range(groups)]
    vall = refs[2 * groups]
    blocks = [refs[2 * groups + 1 + 2 * g : 2 * groups + 3 + 2 * g] for g in range(groups)]
    start = 4 * groups + 1
    panels = refs[start : start + n_panels]
    out = refs[start + n_panels]
    step = pl.program_id(0)

    @pl.when(step == 0)
    def _():
        out[...] = jnp.zeros_like(out)

    done = 0
    for g in range(groups):
        (own, tile), (off, diag) = lists[g], blocks[g]
        images = []
        for i in range(per_step):
            b = step * per_step + i
            left = [
                vall[own[b, k], :, pl.ds(pl.multiple_of(tile[b, k] * BS, BS), BS)] for k in range(TPR)
            ] + [vall[homes[g], :, pl.ds(pl.multiple_of(b * BS, BS), BS)]]
            right = [off[i, k] for k in range(TPR)] + [diag[i]]
            images.append(
                lax.dot_general(
                    jnp.concatenate(left, axis=1),
                    jnp.concatenate(right, axis=1),
                    NT,
                    preferred_element_type=jnp.float32,
                ).astype(jnp.bfloat16)
            )
        image = jnp.concatenate(images, axis=1)
        row = 0
        span = per_step * BS
        pieces = [p[...] for p in panels[done : done + panel_counts[g]]]
        starts = [None] * len(pieces)
        if g == 1:
            share = vall[homes[g], :, pl.ds(pl.multiple_of(step * span, span), span)]
            pieces = [share] + pieces
            size = share.shape[0]
            starts = [homes[2] * size, (1 - homes[2]) * size, 2 * size]
        for values, at in zip(pieces, starts):
            size = values.shape[0]
            place = pl.ds(row if at is None else pl.multiple_of(at, BS), size)
            out[place, :] += lax.dot_general(values, image, NT, preferred_element_type=jnp.float32)
            row += size
        done += panel_counts[g]


def project(homes, lists, vall, blocks, panels, per_step=PER_STEP):
    groups = len(lists)
    local_rows = blocks[0][0].shape[0]
    total = sum(p.shape[0] for p in panels[0])
    smem = pl.BlockSpec(memory_space=pltpu.SMEM)
    span = per_step * BS
    args, specs = [homes], [smem]
    for pair in lists:
        args += pair
        specs += [smem, smem]
    args.append(vall)
    specs.append(pl.BlockSpec(vall.shape, lambda i: (0, 0, 0), pipeline_mode=pl.Buffered(1)))
    for off, diag in blocks:
        args += [off, diag]
        specs += [
            pl.BlockSpec((per_step, TPR, BS, BS), lambda i: (i, 0, 0, 0)),
            pl.BlockSpec((per_step, BS, BS), lambda i: (i, 0, 0)),
        ]
    for group in panels:
        for array in group:
            args.append(array)
            specs.append(pl.BlockSpec((array.shape[0], span), lambda i: (0, i)))
    width = vall.shape[1]
    return pl.pallas_call(
        functools.partial(project_kernel, groups, per_step, tuple(len(g) for g in panels)),
        out_shape=jax.ShapeDtypeStruct((total, width), jnp.float32),
        grid=(local_rows // per_step,),
        in_specs=specs,
        out_specs=pl.BlockSpec((total, width), lambda i: (0, 0)),
        compiler_params=pltpu.CompilerParams(vmem_limit_bytes=48 * MIB),
    )(*args)


def scatter_kernel(n_rows, partial, out, land, send, recv):
    r, c = lax.axis_index("rows"), lax.axis_index("cols")
    x = r % 2
    rows, width = out.shape[0], partial.shape[1]
    barrier = pltpu.get_barrier_semaphore()
    for d in range(1, n_rows):
        pl.semaphore_signal(barrier, inc=1, device_id=((r + d) % n_rows, c), device_id_type=MESH)
    pl.semaphore_wait(barrier, n_rows - 1)

    def share(target):
        per_half = n_rows // 2
        place = (target // per_half + c) % 2 * per_half + target % per_half
        return partial.at[pl.ds(pl.multiple_of(place * rows, rows), rows), :]

    def copy(d):
        target = (r + d) % n_rows
        return pltpu.make_async_remote_copy(
            src_ref=share(target), dst_ref=land.at[d], send_sem=send.at[d], recv_sem=recv.at[d],
            device_id=(target, c), device_id_type=MESH,
        )

    for d in range(1, n_rows):
        copy(d).start()
    mine = share(r)[...]
    other = jnp.zeros_like(mine)
    for d in range(1, n_rows):
        copy(d).wait_recv()
        if d % 2:
            other = other + land[d]
        else:
            mine = mine + land[d]
    first = x == 0
    out[:, pl.ds(0, width)] = jnp.where(first, mine, other)
    out[:, pl.ds(width, width)] = jnp.where(first, other, mine)
    for d in range(1, n_rows):
        copy(d).wait_send()


def scatter(partial):
    n_rows = lax.axis_size("rows")
    rows, width = partial.shape[0] // n_rows, partial.shape[1]
    dma = pltpu.SemaphoreType.DMA
    vmem = pl.BlockSpec(memory_space=pltpu.VMEM)
    return pl.pallas_call(
        functools.partial(scatter_kernel, n_rows),
        out_shape=jax.ShapeDtypeStruct((rows, 2 * width), jnp.float32),
        in_specs=[vmem],
        out_specs=vmem,
        scratch_shapes=[pltpu.VMEM((n_rows, rows, width), jnp.float32), dma((n_rows,)), dma((n_rows,))],
        compiler_params=pltpu.CompilerParams(collective_id=1, has_side_effects=True),
    )(partial)


def on_chip_pairs(basis_t, diag_tiles, off_tiles, owners, tile_block):
    vall, offp, diagp, ownp, tilep, pv0, pvx, pv2 = gather(basis_t, diag_tiles, off_tiles, owners, tile_block)
    r = lax.axis_index("rows")
    x = r % 2
    side = r + 1 - 2 * x
    homes = jnp.stack([r, side, x]).astype(jnp.int32)
    partial = project(
        homes,
        [(owners, tile_block), (ownp, tilep)],
        vall,
        [(off_tiles, diag_tiles), (offp, diagp)],
        [[basis_t, pv0], [pvx, pv2]],
    )
    return scatter(partial)


def general(basis_t, diag_tiles, off_tiles, owners, tile_block):
    vall = lax.all_gather(basis_t, "rows", axis=0, tiled=False)
    whole = lax.all_gather(basis_t, "cols", axis=0, tiled=True)
    homes = lax.axis_index("rows").astype(jnp.int32).reshape(1)
    partial = project(
        homes, [(owners, tile_block)], vall, [(off_tiles, diag_tiles)], [[whole]]
    )
    return lax.psum_scatter(partial, "rows", scatter_dimension=0, tiled=True)


def solution(mesh):
    in_specs = (
        P("cols", "rows"),
        P("rows", None, None),
        P("rows", None, None, None),
        P("rows", None),
        P("rows", None),
    )
    pairs = mesh.shape["cols"] == 2 and mesh.shape["rows"] == 4 * LINE
    return jax.shard_map(
        on_chip_pairs if pairs else general,
        mesh=mesh, in_specs=in_specs, out_specs=P("rows", "cols"), check_vma=False,
    )
```
